128 devices in a mesh: inp: 8 (over z, core), out: 8 (over y_lo, x), dep: 2 (over y_hi).
Axes of the slice: x: 4, y: 4 (y_hi: 2, y_lo: 2; y = y_hi * 2 + y_lo), z: 4, core: 2. Of those that a mesh axis runs over, the one named last changes fastest.
Arguments:
- tokens_in: bfloat16 [1024, 8192], P(('out', 'dep'), 'inp'), may hold values from -6 to 6
- grad_out: bfloat16 [1024, 8192], P(('out', 'dep'), 'inp'), may hold values from -0.59765625 to 0.59765625
- w_gate: bfloat16 [8192, 14336], P('inp', ('out', 'dep')), may hold values from -0.0625 to 0.0625
- w_up: bfloat16 [8192, 14336], P('inp', ('out', 'dep')), may hold values from -0.0625 to 0.0625
- w_down: bfloat16 [14336, 8192], P(('out', 'dep'), 'inp'), may hold values from -0.046875 to 0.046875
Outputs:
- grad_tokens: bfloat16 [1024, 8192], P(('out', 'dep'), 'inp')
- grad_w_gate: bfloat16 [8192, 14336], P('inp', ('out', 'dep'))
- grad_w_up: bfloat16 [8192, 14336], P('inp', ('out', 'dep'))
- grad_w_down: bfloat16 [14336, 8192], P(('out', 'dep'), 'inp')
The draws below stay inside these ranges and needn't reach their ends.
All inputs are finite; a program needn't handle non-finite values.
Results may differ from the reference program's by a relative error of at most 0.034.
Values may be sent and summed in bfloat16 or wider, within the bound.
No kernel may reach another device: no remote copies, remote signals or barrier semaphores. Data moves between devices by JAX's collectives and lax.ppermute only.
A program may use at most 128 MiB of HBM per device.

```python
import jax
import jax.numpy as jnp
from jax import lax

D = 8192
FF = 14336
TOKENS = 1024
N_INP = 8


def level_of(key, dims, shards, low, largest):
    loudness = 1.0
    for position, blocks in shards:
        steps = jax.random.uniform(jax.random.fold_in(jax.random.fold_in(key, 6), position), (blocks,), jnp.float32, low / len(shards), largest / len(shards))
        loudness = loudness * jnp.repeat(jnp.exp(steps), dims[position] // blocks).reshape((-1,) + (1,) * (len(dims) - 1 - position))
    return loudness


def normal_values(key, extent, deviation, bound, pieces=(), held_as=jnp.bfloat16):
    level = level_of(key, extent, pieces, -0.22, 0.18) if pieces else 1.0
    result = jax.random.normal(key, extent, jnp.float32) * deviation * level
    return jnp.minimum(jnp.maximum(result, -bound), bound).astype(held_as)


def setup_inputs(seed: int = 0) -> dict:
    keys = jax.random.split(jax.random.key(seed), 6)
    tokens_in = normal_values(keys[0], (TOKENS, D), 1.0, 6.0, ((0, 16), (1, 8)))
    grad_out = normal_values(keys[1], (TOKENS, D), 0.1, 0.59765625, ((0, 16), (1, 8)))
    w_gate = normal_values(keys[2], (D, FF), D ** -0.5, 0.0625, ((0, 8), (1, 16)))
    w_up = normal_values(keys[3], (D, FF), D ** -0.5, 0.0625, ((0, 8), (1, 16)))
    w_down = normal_values(keys[4], (FF, D), FF ** -0.5, 0.046875, ((0, 16), (1, 8)))
    return dict(tokens_in=tokens_in, grad_out=grad_out, w_gate=w_gate, w_up=w_up, w_down=w_down)


def blocked_product(left, right):
    width = left.shape[1] // N_INP
    total = jnp.zeros((left.shape[0], right.shape[1]), jnp.float32)
    for block in range(N_INP):
        part = jnp.dot(left[:, block * width:(block + 1) * width], right[block * width:(block + 1) * width, :], preferred_element_type=jnp.float32)
        rounded = lax.optimization_barrier(part.astype(jnp.bfloat16))
        total = total + rounded.astype(jnp.float32)
    return total


def reference(tokens_in, grad_out, w_gate, w_up, w_down):
    gate = blocked_product(tokens_in, w_gate)
    up = blocked_product(tokens_in, w_up)
    grad_hidden = blocked_product(grad_out, w_down.T)
    sig = jax.nn.sigmoid(gate)
    silu = gate * sig
    hidden = (silu * up).astype(jnp.bfloat16)
    grad_gate = (grad_hidden * up * sig * (1.0 + gate * (1.0 - sig))).astype(jnp.bfloat16)
    grad_up = (grad_hidden * silu).astype(jnp.bfloat16)
    grad_w_gate = jnp.dot(tokens_in.T, grad_gate, preferred_element_type=jnp.float32).astype(jnp.bfloat16)
    grad_w_up = jnp.dot(tokens_in.T, grad_up, preferred_element_type=jnp.float32).astype(jnp.bfloat16)
    grad_w_down = jnp.dot(hidden.T, grad_out, preferred_element_type=jnp.float32).astype(jnp.bfloat16)
    grad_tokens = jnp.dot(grad_gate, w_gate.T, preferred_element_type=jnp.float32) + jnp.dot(grad_up, w_up.T, preferred_element_type=jnp.float32)
    return grad_tokens.astype(jnp.bfloat16), grad_w_gate, grad_w_up, grad_w_down
```

```python
import functools

import jax
import jax.numpy as jnp
from jax import lax
from jax.experimental import pallas as pl
from jax.experimental.pallas import tpu as pltpu
from jax.sharding import PartitionSpec as P

XY = ("out", "dep")
BF = jnp.bfloat16
F32 = jnp.float32
MB = 1024 * 1024
PIECE = 32
OFFSETS = (0, 1, 3, 2)


def xy_index(x, y):
    return ((y % 2) * 4 + x) * 2 + y // 2


def from_xy(value, dx, dy):
    pairs = [
        (xy_index((x + dx) % 4, (y + dy) % 4), xy_index(x, y)) for x in range(4) for y in range(4)
    ]
    return lax.ppermute(value, XY, pairs)


def from_z(value, dz, dc=0):
    pairs = [
        (((z + dz) % 4) * 2 + (c + dc) % 2, z * 2 + c) for z in range(4) for c in range(2)
    ]
    return lax.ppermute(value, "inp", pairs)


def params(mb):
    return pltpu.CompilerParams(vmem_limit_bytes=mb * MB)


def vmem(n):
    return [pl.BlockSpec(memory_space=pltpu.VMEM)] * n


def place_of(i, per, z, c):
    slot = i // per
    away = lax.rem(slot // 2 - z + 4, 4)
    away = jnp.where(away == 3, 2, jnp.where(away == 2, 3, away))
    other = jnp.where(slot % 2 == c, 0, 1)
    return (other * 4 + away) * per + i % per


def forward_kernel(counts, where, *refs):
    n = len(counts)
    pieces, (wg, wu, wd) = refs[:n], refs[n:n + 3]
    xs, dys, keep, send = refs[n + 3:]
    total = sum(counts)
    per = total // 8
    z, c = where[0], where[1]
    i = 0
    for ref, count in zip(pieces, counts):
        for j in range(count):
            row = pl.multiple_of(place_of(i, per, z, c) * PIECE, PIECE)
            xs[pl.ds(row, PIECE), :] = ref[j, 0]
            dys[pl.ds(row, PIECE), :] = ref[j, 1]
            i += 1
    t = per * PIECE
    rows = 256
    for half, out in ((1, send), (0, keep)):
        half_rows = 4 * t
        step = min(rows, half_rows)
        for r in range(half_rows // step):
            at = half * half_rows + r * step
            a = xs[pl.ds(at, step), :]
            b = dys[pl.ds(at, step), :]
            gate = jnp.dot(a, wg[...], preferred_element_type=F32).astype(BF)
            up = jnp.dot(a, wu[...], preferred_element_type=F32).astype(BF)
            back = lax.dot_general(b, wd[...], (((1,), (1,)), ((), ())), preferred_element_type=F32).astype(BF)
            blocks = step // t
            for k in range(blocks):
                for m, v in enumerate((gate, up, back)):
                    out[r * blocks + k, m] = v[k * t:(k + 1) * t]


def forward(where, pieces, wg, wu, wd):
    counts = tuple(p.shape[0] for p in pieces)
    per = sum(counts) // 8
    t = per * PIECE
    f = wg.shape[1]
    d = wg.shape[0]
    block = jax.ShapeDtypeStruct((4, 3, t, f), BF)
    rows = jax.ShapeDtypeStruct((8 * t, d), BF)
    return pl.pallas_call(
        functools.partial(forward_kernel, counts),
        out_shape=(rows, rows, block, block),
        in_specs=[pl.BlockSpec(memory_space=pltpu.SMEM)] + vmem(len(pieces) + 3),
        out_specs=vmem(4),
        compiler_params=params(48),
        cost_estimate=pl.CostEstimate(flops=6 * 8 * t * d * f, bytes_accessed=6 * d * f + 16 * t * d * 4, transcendentals=0),
        name="forward",
    )(where, *pieces, wg, wu, wd)


def add_cores_kernel(keep, got, b0, b1, b2, h0, h1):
    t = b0.shape[1]

    def add(k):
        return keep[k].astype(F32) + got[k].astype(F32)

    b0[...] = add(0)
    b1[...] = add(1).astype(BF)
    b2[...] = add(2).astype(BF)
    far = add(3).astype(BF)
    h0[...] = far[:, : t // 2]
    h1[...] = far[:, t // 2:]


def add_cores(keep, got):
    _, _, t, f = keep.shape
    whole = jax.ShapeDtypeStruct((3, t, f), BF)
    half = jax.ShapeDtypeStruct((3, t // 2, f), BF)
    return pl.pallas_call(
        add_cores_kernel,
        out_shape=(jax.ShapeDtypeStruct((3, t, f), F32), whole, whole, half, half),
        in_specs=vmem(2),
        out_specs=vmem(5),
        compiler_params=params(32),
        name="add_cores",
    )(keep, got)


def add_far_kernel(b1, b2, r0, r1, o1, o2):
    t = b1.shape[1]
    o1[:, : t // 2] = (b1[:, : t // 2].astype(F32) + r0[...].astype(F32)).astype(BF)
    o1[:, t // 2:] = b1[:, t // 2:]
    o2[:, : t // 2] = b2[:, : t // 2]
    o2[:, t // 2:] = (b2[:, t // 2:].astype(F32) + r1[...].astype(F32)).astype(BF)


def add_far(b1, b2, r0, r1):
    whole = jax.ShapeDtypeStruct(b1.shape, BF)
    return pl.pallas_call(
        add_far_kernel,
        out_shape=(whole, whole),
        in_specs=vmem(4),
        out_specs=vmem(2),
        compiler_params=params(32),
        name="add_far",
    )(b1, b2, r0, r1)


def activate_kernel(b0, q1, q2, out):
    sums = [b0[m] + q1[m].astype(F32) + q2[m].astype(F32) for m in range(3)]
    gate, up, back = sums
    sig = 1.0 / (1.0 + jnp.exp(-gate))
    silu = gate * sig
    out[0] = (silu * up).astype(BF)
    out[1] = (back * up * sig * (1.0 + gate * (1.0 - sig))).astype(BF)
    out[2] = (back * silu).astype(BF)


def activate(b0, q1, q2):
    return pl.pallas_call(
        activate_kernel,
        out_shape=jax.ShapeDtypeStruct(b0.shape, BF),
        in_specs=vmem(3),
        out_specs=vmem(1)[0],
        compiler_params=params(32),
        name="activate",
    )(b0, q1, q2)


def backward_kernel(counts, targets, where, mine, theirs, wg, wu, hidden, both, sums, gg, gu, res):
    per = sum(counts) // 8
    _, _, t, f = mine.shape
    for half, ref in ((0, mine), (1, theirs)):
        for k in range(4):
            at = (half * 4 + k) * t
            hidden[at:at + t, :] = ref[k, 0]
            both[at:at + t, :f] = ref[k, 1]
            both[at:at + t, f:] = ref[k, 2]
    rows = 256
    dims = (((1,), (1,)), ((), ()))
    for r in range(8 * t // rows):
        part = slice(r * rows, (r + 1) * rows)
        value = lax.dot_general(both[part, :f], wg[...], dims, preferred_element_type=F32)
        value = value + lax.dot_general(both[part, f:], wu[...], dims, preferred_element_type=F32)
        res[part, :] = value.astype(BF)
    z, c = where[0], where[1]
    x, y = where[2], where[3]
    for i, (dx, dy, lo) in enumerate(targets):
        xx = lax.rem(x + dx, 4)
        yy = lax.rem(y + dy, 4)
        device = (lax.rem(yy, 2) * 4 + xx) * 2 + yy // 2
        row = pl.multiple_of(place_of(i, per, z, c) * PIECE, PIECE)
        sums[device, lo:lo + PIECE, :] = res[pl.ds(row, PIECE), :]


def backward(where, mine, theirs, wg, wu, counts, targets):
    _, _, t, f = mine.shape
    d = wg.shape[0]
    return pl.pallas_call(
        functools.partial(backward_kernel, counts, targets),
        out_shape=(
            jax.ShapeDtypeStruct((8 * t, f), BF),
            jax.ShapeDtypeStruct((8 * t, 2 * f), BF),
            jax.ShapeDtypeStruct((16, 2 * PIECE, d), BF),
        ),
        in_specs=[pl.BlockSpec(memory_space=pltpu.SMEM)] + vmem(4),
        out_specs=vmem(3),
        scratch_shapes=[pltpu.VMEM((8, 128), BF), pltpu.VMEM((8, 128), BF), pltpu.VMEM((8 * t, d), BF)],
        compiler_params=params(48),
        cost_estimate=pl.CostEstimate(flops=4 * 8 * t * d * f, bytes_accessed=4 * d * f + 8 * t * (6 * f + 2 * d), transcendentals=0),
        name="backward",
    )(where, mine, theirs, wg, wu)


def weights_kernel(xs, dys, hidden, both, o_gate, o_up, o_down, turned):
    f = o_gate.shape[1]
    dims = (((0,), (0,)), ((), ()))

    @pl.when(pl.program_id(0) == 0)
    def _():
        turned[...] = hidden[...].T

    value = lax.dot_general(xs[...], both[...], dims, preferred_element_type=F32).astype(BF)
    o_gate[...] = value[:, :f]
    o_up[...] = value[:, f:]
    o_down[...] = jnp.dot(turned[...], dys[...], preferred_element_type=F32).astype(BF)


def weights(xs, dys, hidden, both):
    tokens, d = xs.shape
    f = hidden.shape[1]
    n = 4
    w = d // n
    return pl.pallas_call(
        weights_kernel,
        grid=(n,),
        out_shape=(
            jax.ShapeDtypeStruct((d, f), BF),
            jax.ShapeDtypeStruct((d, f), BF),
            jax.ShapeDtypeStruct((f, d), BF),
        ),
        in_specs=[
            pl.BlockSpec((tokens, w), lambda i: (0, i)),
            pl.BlockSpec((tokens, w), lambda i: (0, i)),
            pl.BlockSpec((tokens, f), lambda i: (0, 0)),
            pl.BlockSpec((tokens, 2 * f), lambda i: (0, 0)),
        ],
        out_specs=[
            pl.BlockSpec((w, f), lambda i: (i, 0)),
            pl.BlockSpec((w, f), lambda i: (i, 0)),
            pl.BlockSpec((f, w), lambda i: (0, i)),
        ],
        scratch_shapes=[pltpu.VMEM((f, tokens), BF)],
        compiler_params=params(48),
        cost_estimate=pl.CostEstimate(flops=6 * tokens * d * f, bytes_accessed=6 * d * f + tokens * (4 * d + 6 * f), transcendentals=0),
        name="weights",
    )(xs, dys, hidden, both)


def gather_plane(first, second):
    def along(value, swap, a, b=0):
        return from_xy(value, *((b, a) if swap else (a, b)))

    lines = []
    for value, swap in ((first, False), (second, True)):
        lines.append([value] + [along(value, swap, o) for o in OFFSETS[1:]])
    lines = [jnp.stack(line) for line in lines]
    near = []
    for line, swap in zip(lines, (False, True)):
        near.append((along(line, not swap, 1), along(line, not swap, -1)))
    far = []
    for (ahead, behind), swap in zip(near, (False, True)):
        far.append((along(ahead[:2], not swap, 1), along(behind[2:], not swap, -1)))
    pieces, targets = [], []

    def put(array, which, step, parts):
        pieces.append(array)
        for j in parts:
            one, two = OFFSETS[j], step % 4
            targets.append((one, two, 0) if which == 0 else (two, one, PIECE))

    for which in range(2):
        put(lines[which], which, 0, range(4))
    for which in range(2):
        put(near[which][0], which, 1, range(4))
        put(near[which][1], which, -1, range(4))
    for which in range(2):
        put(far[which][0], which, 2, (0, 1))
        put(far[which][1], which, 2, (2, 3))
    return pieces, tuple(targets)


def local(tokens_in, grad_out, w_gate, w_up, w_down):
    inp, out, dep = (lax.axis_index(a) for a in ("inp", "out", "dep"))
    where = jnp.stack([inp // 2, inp % 2, out % 4, dep * 2 + out // 4]).astype(jnp.int32)
    own = jnp.stack([tokens_in, grad_out])
    pieces, targets = gather_plane(own[:, :PIECE], own[:, PIECE:])
    counts = tuple(p.shape[0] for p in pieces)

    xs, dys, keep, send = forward(where, pieces, w_gate, w_up, w_down)
    b0, b1, b2, h0, h1 = add_cores(keep, from_z(send, 0, 1))
    t = b0.shape[1]
    b1, b2 = add_far(b1, b2, from_z(h0, -1), from_z(h1, 1))
    trio = activate(b0, from_z(b1, -1), from_z(b2, 1))
    ahead, behind = from_z(trio, 1), from_z(trio, -1)
    far = jnp.concatenate([from_z(behind[:, : t // 2], -1), from_z(ahead[:, t // 2:], 1)], axis=1)
    mine = jnp.stack([trio, ahead, behind, far])
    theirs = from_z(mine, 0, 1)
    hidden, both, sums = backward(where, mine, theirs, w_gate, w_up, counts, targets)
    parts = lax.all_to_all(sums, XY, 0, 0)
    grad_w_gate, grad_w_up, grad_w_down = weights(xs, dys, hidden, both)
    grad_tokens = jnp.sum(parts.astype(F32), axis=0).astype(BF)
    return grad_tokens, grad_w_gate, grad_w_up, grad_w_down


def solution(mesh):
    return jax.shard_map(
        local,
        mesh=mesh,
        in_specs=(P(XY, "inp"), P(XY, "inp"), P("inp", XY), P("inp", XY), P(XY, "inp")),
        out_specs=(P(XY, "inp"), P("inp", XY), P("inp", XY), P(XY, "inp")),
        check_vma=False,
    )
```

```python
import functools

import jax
import jax.numpy as jnp
from jax import lax
from jax.experimental import pallas as pl
from jax.experimental.pallas import tpu as pltpu
from jax.sharding import PartitionSpec as P

XY = ("out", "dep")
ALL = ("inp", "out", "dep")
BF = jnp.bfloat16
F32 = jnp.float32
MB = 1024 * 1024
PIECE = 32
OFFSETS = (0, 1, 3, 2)
ROWS = (((0,), (0,)), ((), ()))
LANES = (((1,), (1,)), ((), ()))


def index(x, y, z, c):
    return (z * 2 + c) * 16 + ((y % 2) * 4 + x) * 2 + y // 2


def from_where(value, shift):
    pairs = []
    for x in range(4):
        for y in range(4):
            for z in range(4):
                for c in range(2):
                    a, b, d, e = shift(x, y, z, c)
                    pairs.append((index(a % 4, b % 4, d % 4, e % 2), index(x, y, z, c)))
    return lax.ppermute(value, ALL, pairs)


def from_line(value, step):
    return from_where(value, lambda x, y, z, c: (x + (step if c == 0 else 0), y + (step if c == 1 else 0), z, c))


def from_side(value, step):
    return from_where(value, lambda x, y, z, c: (x + (step if c == 1 else 0), y + (step if c == 0 else 0), z, c))


def from_z(value, step):
    return from_where(value, lambda x, y, z, c: (x, y, z + step, c))


def from_core(value):
    return from_where(value, lambda x, y, z, c: (x, y, z, c + 1))


def params(mb=48):
    return pltpu.CompilerParams(vmem_limit_bytes=mb * MB)


def vmem(n):
    return [pl.BlockSpec(memory_space=pltpu.VMEM)] * n


def shape(*dims, dtype=BF):
    return jax.ShapeDtypeStruct(dims, dtype)


def hbm(arrays):
    return [pltpu.with_memory_space_constraint(a, pltpu.HBM) for a in arrays]


SMEM = pl.BlockSpec(memory_space=pltpu.SMEM)


def place_of(i, per, z):
    if z is None:
        return i * PIECE
    away = lax.rem(i // per - z + 4, 4)
    away = jnp.where(away == 3, 2, jnp.where(away == 2, 3, away))
    return pl.multiple_of((away * per + i % per) * PIECE, PIECE)


def forward_kernel(counts, ring, where, *refs):
    n = len(counts)
    pieces, mine, other = refs[:n], refs[n:n + 3], refs[n + 3:n + 6]
    rows_mine, rows_other, *outs, rows, wide, down, sems = refs[n + 6:]
    held = wide.at[0], wide.at[1], wide.at[2], wide.at[3], down.at[0], down.at[1]
    per = sum(counts) // 4
    t = per * PIECE
    moves = []
    for ref, count in zip(pieces, counts):
        for j in range(count):
            row = place_of(len(moves), per, where[0] if ring else None)
            moves.append((ref.at[j], rows.at[:, :, pl.ds(row, PIECE), :]))
    total = len(moves)
    moves += list(zip((mine[0], other[0], mine[1], other[1], mine[2], other[2]), held))
    copies = [pltpu.make_async_copy(a, b, sems.at[k]) for k, (a, b) in enumerate(moves)]
    for copy in copies:
        copy.start()
    for copy in copies[:total]:
        copy.wait()
    copies = copies[total:]
    results = [pltpu.make_async_copy(rows.at[k], out, sems.at[k]) for k, out in enumerate((rows_mine, rows_other))]
    for copy in results:
        copy.start()
    for m in range(3):
        src = 0 if m < 2 else 1
        dims = (((1,), (0,)), ((), ())) if m < 2 else LANES
        copies[2 * m].wait()
        copies[2 * m + 1].wait()
        v = lax.dot_general(rows[0, src], held[2 * m][...], dims, preferred_element_type=F32)
        v = v + lax.dot_general(rows[1, src], held[2 * m + 1][...], dims, preferred_element_type=F32)
        v = v.astype(BF)
        for block in range(4):
            part = v[block * t:(block + 1) * t]
            if not ring:
                outs[0][block, m] = part
            elif block < 3:
                outs[block][m] = part
            else:
                outs[3][m] = part[: t // 2]
                outs[4][m] = part[t // 2:]
    for copy in results:
        copy.wait()


def forward(where, pieces, mine, other, ring):
    counts = tuple(p.shape[0] for p in pieces)
    t = sum(counts) // 4 * PIECE
    d, f = mine[0].shape
    rows = pltpu.HBM((2, 4 * t, d), BF)
    whole, half = shape(3, t, f), shape(3, t // 2, f)
    outs = (whole, whole, whole, half, half) if ring else (shape(4, 3, t, f),)
    far = [pl.BlockSpec(memory_space=pltpu.HBM)]
    return pl.pallas_call(
        functools.partial(forward_kernel, counts, ring),
        out_shape=(rows, rows, *outs),
        in_specs=[SMEM] + far * (len(pieces) + 6),
        out_specs=far * 2 + vmem(len(outs)),
        scratch_shapes=[
            pltpu.VMEM((2, 2, 4 * t, d), BF),
            pltpu.VMEM((4, d, f), BF),
            pltpu.VMEM((2, f, d), BF),
            pltpu.SemaphoreType.DMA((sum(counts) + 6,)),
        ],
        compiler_params=params(18 + 16 * t // 256),
        cost_estimate=pl.CostEstimate(flops=12 * 4 * t * d * f, bytes_accessed=12 * d * f + 64 * t * d, transcendentals=0),
        name="forward",
    )(where, *hbm(pieces), *hbm(mine), *hbm(other))


def add_far_kernel(b1, b2, r0, r1, o1, o2):
    t = b1.shape[1]
    o1[:, : t // 2] = (b1[:, : t // 2].astype(F32) + r0[...].astype(F32)).astype(BF)
    o1[:, t // 2:] = b1[:, t // 2:]
    o2[:, : t // 2] = b2[:, : t // 2]
    o2[:, t // 2:] = (b2[:, t // 2:].astype(F32) + r1[...].astype(F32)).astype(BF)


def add_far(b1, b2, r0, r1):
    return pl.pallas_call(
        add_far_kernel,
        out_shape=(shape(*b1.shape), shape(*b1.shape)),
        in_specs=vmem(4),
        out_specs=vmem(2),
        compiler_params=params(8),
        name="add_far",
    )(b1, b2, r0, r1)


def activate_kernel(n, *refs):
    parts, outs = refs[:n], refs[n:]

    def total(m):
        if n == 1:
            return sum(parts[0][k, m].astype(F32) for k in range(4))
        return sum(p[m].astype(F32) for p in parts)

    gate, up, back = (total(m) for m in range(3))
    sig = 1.0 / (1.0 + jnp.exp(-gate))
    silu = gate * sig
    values = (silu * up, back * up * sig * (1.0 + gate * (1.0 - sig)), back * silu)
    for m, v in enumerate(values):
        v = v.astype(BF)
        if n == 1:
            for k in range(4):
                outs[0][k, m] = v
        else:
            outs[0][m] = v


def activate(*parts):
    return pl.pallas_call(
        functools.partial(activate_kernel, len(parts)),
        out_shape=shape(*parts[0].shape),
        in_specs=vmem(len(parts)),
        out_specs=vmem(1)[0],
        compiler_params=params(8),
        name="activate",
    )(*parts)


def assemble_kernel(n, *refs):
    out = refs[n]
    if n == 1:
        t = refs[0].shape[2]
        for k in range(4):
            for m in range(3):
                out[m, k * t:(k + 1) * t] = refs[0][k, m]
        return
    t = refs[0].shape[1]
    for k in range(3):
        out[:, k * t:(k + 1) * t] = refs[k][...]
    out[:, 3 * t:3 * t + t // 2] = refs[3][...]
    out[:, 3 * t + t // 2:] = refs[4][...]


def assemble(*parts):
    *_, t, f = parts[0].shape
    return pl.pallas_call(
        functools.partial(assemble_kernel, len(parts)),
        out_shape=shape(3, 4 * t, f),
        in_specs=vmem(len(parts)),
        out_specs=vmem(1)[0],
        compiler_params=params(12),
        name="assemble",
    )(*parts)


def backward_kernel(counts, ring, where, trio, *refs):
    mine, other = refs[:2], refs[2:4]
    outs, (res, held, sems) = refs[4:-3], refs[-3:]
    copies = [pltpu.make_async_copy(w, held.at[k], sems.at[k]) for k, w in enumerate((*mine, *other))]
    for copy in copies:
        copy.start()
    per = sum(counts) // 4
    for b in range(2):
        copies[2 * b].wait()
        v = lax.dot_general(trio[1], held[2 * b], LANES, preferred_element_type=F32)
        copies[2 * b + 1].wait()
        v = v + lax.dot_general(trio[2], held[2 * b + 1], LANES, preferred_element_type=F32)
        res[b] = v.astype(BF)
    i = 0
    for ref, count in zip(outs, counts):
        for j in range(count):
            row = place_of(i, per, where[0] if ring else None)
            for b in range(2):
                ref[j, b] = res[b, pl.ds(row, PIECE), :]
            i += 1


def backward(where, trio, mine, other, counts, ring):
    _, tokens, f = trio.shape
    d = mine[0].shape[0]
    return pl.pallas_call(
        functools.partial(backward_kernel, counts, ring),
        out_shape=tuple(shape(n, 2, PIECE, d) for n in counts),
        in_specs=[SMEM] + vmem(1) + [pl.BlockSpec(memory_space=pltpu.HBM)] * 4,
        out_specs=tuple(vmem(len(counts))),
        scratch_shapes=[pltpu.VMEM((2, tokens, d), BF), pltpu.VMEM((4, d, f), BF), pltpu.SemaphoreType.DMA((4,))],
        compiler_params=params(12 + 14 * tokens // 512),
        cost_estimate=pl.CostEstimate(flops=8 * tokens * d * f, bytes_accessed=8 * d * f + tokens * (6 * f + 4 * d), transcendentals=0),
        name="backward",
    )(where, trio, *mine[:2], *other[:2])


def weights_kernel(n, *refs):
    rows, trios = refs[:n], refs[n:2 * n]
    o_gate, o_up, x, both = refs[2 * n:]
    f = o_gate.shape[1]

    @pl.when(pl.program_id(0) == 0)
    def _():
        at = 0
        for ref in trios:
            k = ref.shape[1]
            both[at:at + k, :f] = ref[0]
            both[at:at + k, f:] = ref[1]
            at += k

    at = 0
    for ref in rows:
        k = ref.shape[1]
        x[at:at + k, :] = ref[0]
        at += k
    value = lax.dot_general(x[...], both[...], ROWS, preferred_element_type=F32).astype(BF)
    o_gate[...] = value[:, :f]
    o_up[...] = value[:, f:]


def weights(rows, trios):
    n = len(rows)
    d, f = rows[0].shape[2], trios[0].shape[2]
    tokens = sum(t.shape[1] for t in trios)
    w = 512
    return pl.pallas_call(
        functools.partial(weights_kernel, n),
        grid=(d // w,),
        out_shape=(shape(d, f), shape(d, f)),
        in_specs=[pl.BlockSpec((1, r.shape[1], w), lambda i: (0, 0, i)) for r in rows]
        + [pl.BlockSpec((pl.Element(2, (0, 0)), pl.Element(t.shape[1]), pl.Element(f)), lambda i: (1, 0, 0)) for t in trios],
        out_specs=[pl.BlockSpec((w, f), lambda i: (i, 0))] * 2,
        scratch_shapes=[pltpu.VMEM((tokens, w), BF), pltpu.VMEM((tokens, 2 * f), BF)],
        compiler_params=params(32),
        cost_estimate=pl.CostEstimate(flops=4 * tokens * d * f, bytes_accessed=4 * d * f + tokens * (2 * d + 4 * f), transcendentals=0),
        name="weights",
    )(*rows, *trios)


def down_kernel(n, *refs):
    rows, trios = refs[:n], refs[n:2 * n]
    o_down, y, turned = refs[2 * n:]

    @pl.when(pl.program_id(0) == 0)
    def _():
        at = 0
        for ref in trios:
            k = ref.shape[1]
            turned[:, at:at + k] = ref[0].T
            at += k

    at = 0
    for ref in rows:
        k = ref.shape[1]
        y[at:at + k, :] = ref[0]
        at += k
    o_down[...] = jnp.dot(turned[...], y[...], preferred_element_type=F32).astype(BF)


def down_weights(rows, trios):
    n = len(rows)
    d, f = rows[0].shape[2], trios[0].shape[2]
    tokens = sum(t.shape[1] for t in trios)
    w = 512
    return pl.pallas_call(
        functools.partial(down_kernel, n),
        grid=(d // w,),
        out_shape=shape(f, d),
        in_specs=[pl.BlockSpec((1, r.shape[1], w), lambda i: (1, 0, i)) for r in rows]
        + [pl.BlockSpec((1, t.shape[1], f), lambda i: (0, 0, 0)) for t in trios],
        out_specs=pl.BlockSpec((f, w), lambda i: (0, i)),
        scratch_shapes=[pltpu.VMEM((tokens, w), BF), pltpu.VMEM((f, tokens), BF)],
        compiler_params=params(32),
        cost_estimate=pl.CostEstimate(flops=2 * tokens * d * f, bytes_accessed=2 * d * f + tokens * (2 * d + 2 * f), transcendentals=0),
        name="down_weights",
    )(*rows, *trios)


def plus(a, *rest):
    total = a.astype(F32)
    for b in rest:
        total = total + b.astype(F32)
    return total


def after(value, *others):
    return lax.optimization_barrier((value, others))[0]


def to_all_z(value):
    return lax.all_to_all(value, "inp", 0, 0, axis_index_groups=[[0, 2, 4, 6], [1, 3, 5, 7]])


def local(tokens_in, grad_out, w_gate, w_up, w_down):
    inp = lax.axis_index("inp")
    core = inp % 2
    where = jnp.stack([inp // 2]).astype(jnp.int32)
    mine = (w_gate, w_up, w_down)

    own = jnp.stack([tokens_in, grad_out])
    kept = lax.dynamic_slice_in_dim(own, core * PIECE, PIECE, axis=1)
    given = lax.dynamic_slice_in_dim(own, (1 - core) * PIECE, PIECE, axis=1)
    piece = jnp.stack([kept, from_core(given)])
    line = jnp.stack([piece] + [from_line(piece, o) for o in OFFSETS[1:]])
    other = tuple(from_core(w) for w in after(mine, line))
    ahead, behind = from_side(line, 1), from_side(line, -1)
    far = from_side(ahead[:2], 1), from_side(behind[2:], -1)

    near_pieces = (line, ahead, behind)
    near_mine, near_other, b0, b1, b2, h0, h1 = forward(where, near_pieces, mine, other, True)
    r0, r1 = from_z(h0, -1), from_z(h1, 1)
    far_mine, far_other, parts = forward(where, far, mine, other, False)
    r0, r1 = after((r0, r1), parts)
    sums_far = to_all_z(parts)
    b1, b2 = add_far(b1, b2, r0, r1)
    q1, q2 = from_z(b1, -1), from_z(b2, 1)
    near_got, far_got = from_core(near_other), from_core(far_other)
    trio_far = activate(sums_far)
    q1, q2 = after((q1, q2), trio_far)
    trio = activate(b0, q1, q2)
    t = trio.shape[1]
    up, down = from_z(trio, 1), from_z(trio, -1)
    trio_far = assemble(to_all_z(trio_far))
    trio_far_got = from_core(trio_far)
    up, down = after((up, down), trio_far)
    far0, far1 = backward(where, trio_far, mine, other, (2, 2), False)
    up, down = after((up, down), (far0, far1))
    far0, far1 = from_side(far0, -1), from_side(far1, 1)
    trio = assemble(trio, up, down, from_z(down[:, : t // 2], -1), from_z(up[:, t // 2:], 1))
    trio_got = from_core(trio)
    line, ahead, behind = backward(where, trio, mine, other, (4, 4, 4), True)

    ahead = jnp.concatenate([plus(ahead[:2], far0).astype(BF), ahead[2:]])
    behind = jnp.concatenate([behind[:2], plus(behind[2:], far1).astype(BF)])
    ahead, behind = from_side(ahead, -1), from_side(behind, 1)

    rows = near_mine, far_mine, near_got, far_got
    trios = trio, trio_far, trio_got, trio_far_got
    gate_up = weights(rows, trios)
    ahead, behind = after((ahead, behind), gate_up)

    line = plus(line, ahead, behind)
    sent = [from_line(line[j].astype(BF), -OFFSETS[j]) for j in range(1, 4)]
    grad_w_down = down_weights(rows, trios)
    sent = after(sent, grad_w_down)
    sums = plus(line[0], *sent).astype(BF)
    got = from_core(sums[1])
    first = core == 0
    grad_tokens = jnp.concatenate([jnp.where(first, sums[0], got), jnp.where(first, got, sums[0])])
    return (grad_tokens, *gate_up, grad_w_down)


def solution(mesh):
    return jax.shard_map(
        local,
        mesh=mesh,
        in_specs=(P(XY, "inp"), P(XY, "inp"), P("inp", XY), P("inp", XY), P(XY, "inp")),
        out_specs=(P(XY, "inp"), P("inp", XY), P("inp", XY), P(XY, "inp")),
        check_vma=False,
    )
```

```python
import functools

import jax
import jax.numpy as jnp
from jax import lax
from jax.experimental import pallas as pl
from jax.experimental.pallas import tpu as pltpu
from jax.sharding import PartitionSpec as P

XY = ("out", "dep")
ALL = ("inp", "out", "dep")
BF = jnp.bfloat16
F32 = jnp.float32
MB = 1024 * 1024
PIECE = 32
OFFSETS = (0, 1, 3, 2)
ROWS = (((0,), (0,)), ((), ()))
LANES = (((1,), (1,)), ((), ()))


def index(x, y, z, c):
    return (z * 2 + c) * 16 + ((y % 2) * 4 + x) * 2 + y // 2


def from_where(value, shift):
    pairs = []
    for x in range(4):
        for y in range(4):
            for z in range(4):
                for c in range(2):
                    a, b, d, e = shift(x, y, z, c)
                    pairs.append((index(a % 4, b % 4, d % 4, e % 2), index(x, y, z, c)))
    return lax.ppermute(value, ALL, pairs)


def from_line(value, step):
    return from_where(value, lambda x, y, z, c: (x + (step if c == 0 else 0), y + (step if c == 1 else 0), z, c))


def from_side(value, step):
    return from_where(value, lambda x, y, z, c: (x + (step if c == 1 else 0), y + (step if c == 0 else 0), z, c))


def from_z(value, step):
    return from_where(value, lambda x, y, z, c: (x, y, z + step, c))


def from_core(value):
    return from_where(value, lambda x, y, z, c: (x, y, z, c + 1))


def params(mb=48):
    return pltpu.CompilerParams(vmem_limit_bytes=mb * MB)


def vmem(n):
    return [pl.BlockSpec(memory_space=pltpu.VMEM)] * n


def shape(*dims, dtype=BF):
    return jax.ShapeDtypeStruct(dims, dtype)


def hbm(arrays):
    return [pltpu.with_memory_space_constraint(a, pltpu.HBM) for a in arrays]


SMEM = pl.BlockSpec(memory_space=pltpu.SMEM)


def place_of(i, per, z):
    if z is None:
        return i * PIECE
    away = lax.rem(i // per - z + 4, 4)
    away = jnp.where(away == 3, 2, jnp.where(away == 2, 3, away))
    return pl.multiple_of((away * per + i % per) * PIECE, PIECE)


def forward_kernel(counts, ring, where, *refs):
    n = len(counts)
    pieces, mine, other = refs[:n], refs[n:n + 3], refs[n + 3:n + 6]
    rows_mine, rows_other, *outs, rows, wide, down, sems = refs[n + 6:]
    held = wide.at[0], wide.at[1], wide.at[2], wide.at[3], down.at[0], down.at[1]
    per = sum(counts) // 4
    t = per * PIECE
    moves = []
    for ref, count in zip(pieces, counts):
        for j in range(count):
            row = place_of(len(moves), per, where[0] if ring else None)
            moves.append((ref.at[j], rows.at[:, :, pl.ds(row, PIECE), :]))
    total = len(moves)
    moves += list(zip((mine[0], other[0], mine[1], other[1], mine[2], other[2]), held))
    copies = [pltpu.make_async_copy(a, b, sems.at[k]) for k, (a, b) in enumerate(moves)]
    for copy in copies:
        copy.start()
    for copy in copies[:total]:
        copy.wait()
    copies = copies[total:]
    results = [pltpu.make_async_copy(rows.at[k], out, sems.at[k]) for k, out in enumerate((rows_mine, rows_other))]
    for m in range(3):
        src = 0 if m < 2 else 1
        dims = (((1,), (0,)), ((), ())) if m < 2 else LANES
        copies[2 * m].wait()
        v = lax.dot_general(rows[0, src], held[2 * m][...], dims, preferred_element_type=F32)
        copies[2 * m + 1].wait()
        if m == 2:
            for copy in results:
                copy.start()
        v = v + lax.dot_general(rows[1, src], held[2 * m + 1][...], dims, preferred_element_type=F32)
        v = v.astype(BF)
        for block in range(4):
            part = v[block * t:(block + 1) * t]
            if not ring:
                outs[0][block, m] = part
            elif block < 3:
                outs[block][m] = part
            else:
                outs[3][m] = part[: t // 2]
                outs[4][m] = part[t // 2:]
    for copy in results:
        copy.wait()


def forward(where, pieces, mine, other, ring):
    counts = tuple(p.shape[0] for p in pieces)
    t = sum(counts) // 4 * PIECE
    d, f = mine[0].shape
    rows = pltpu.HBM((2, 4 * t, d), BF)
    whole, half = shape(3, t, f), shape(3, t // 2, f)
    outs = (whole, whole, whole, half, half) if ring else (shape(4, 3, t, f),)
    far = [pl.BlockSpec(memory_space=pltpu.HBM)]
    return pl.pallas_call(
        functools.partial(forward_kernel, counts, ring),
        out_shape=(rows, rows, *outs),
        in_specs=[SMEM] + far * (len(pieces) + 6),
        out_specs=far * 2 + vmem(len(outs)),
        scratch_shapes=[
            pltpu.VMEM((2, 2, 4 * t, d), BF),
            pltpu.VMEM((4, d, f), BF),
            pltpu.VMEM((2, f, d), BF),
            pltpu.SemaphoreType.DMA((sum(counts) + 6,)),
        ],
        compiler_params=params(18 + 16 * t // 256),
        cost_estimate=pl.CostEstimate(flops=12 * 4 * t * d * f, bytes_accessed=12 * d * f + 64 * t * d, transcendentals=0),
        name="forward",
    )(where, *hbm(pieces), *hbm(mine), *hbm(other))


def add_far_kernel(b1, b2, r0, r1, o1, o2):
    t = b1.shape[1]
    o1[:, : t // 2] = (b1[:, : t // 2].astype(F32) + r0[...].astype(F32)).astype(BF)
    o1[:, t // 2:] = b1[:, t // 2:]
    o2[:, : t // 2] = b2[:, : t // 2]
    o2[:, t // 2:] = (b2[:, t // 2:].astype(F32) + r1[...].astype(F32)).astype(BF)


def add_far(b1, b2, r0, r1):
    return pl.pallas_call(
        add_far_kernel,
        out_shape=(shape(*b1.shape), shape(*b1.shape)),
        in_specs=vmem(4),
        out_specs=vmem(2),
        compiler_params=params(8),
        name="add_far",
    )(b1, b2, r0, r1)


def activate_kernel(n, *refs):
    parts, outs = refs[:n], refs[n:]

    def total(m):
        if n == 1:
            return sum(parts[0][k, m].astype(F32) for k in range(4))
        return sum(p[m].astype(F32) for p in parts)

    gate, up, back = (total(m) for m in range(3))
    sig = 1.0 / (1.0 + jnp.exp(-gate))
    silu = gate * sig
    values = (silu * up, back * up * sig * (1.0 + gate * (1.0 - sig)), back * silu)
    for m, v in enumerate(values):
        v = v.astype(BF)
        if n == 1:
            for k in range(4):
                outs[0][k, m] = v
        else:
            outs[0][m] = v


def activate(*parts):
    return pl.pallas_call(
        functools.partial(activate_kernel, len(parts)),
        out_shape=shape(*parts[0].shape),
        in_specs=vmem(len(parts)),
        out_specs=vmem(1)[0],
        compiler_params=params(8),
        name="activate",
    )(*parts)


def gradient_terms(trio, rows, held, copies, res):
    for b in range(2):
        copies[2 * b].wait()
        v = lax.dot_general(trio[1], held[2 * b], LANES, preferred_element_type=F32)
        copies[2 * b + 1].wait()
        v = v + lax.dot_general(trio[2], held[2 * b + 1], LANES, preferred_element_type=F32)
        res[b, rows] = v.astype(BF)


def start_all(sources, targets, sems):
    copies = [pltpu.make_async_copy(a, targets.at[k], sems.at[k]) for k, a in enumerate(sources)]
    for copy in copies:
        copy.start()
    return copies


def hand_out(counts, place, res, outs):
    i = 0
    for ref, count in zip(outs, counts):
        for j in range(count):
            row = place(i)
            for b in range(2):
                ref[j, b] = res[b, pl.ds(row, PIECE), :]
            i += 1


def backward_kernel(counts, parts, *refs):
    copies = start_all(refs[:4], refs[-2], refs[-1])
    trio, outs, res = refs[4], refs[5:-3], refs[-3]
    t = parts.shape[2]
    for k in range(4):
        for m in range(3):
            trio[m, k * t:(k + 1) * t] = parts[k, m]
    gradient_terms(trio, slice(0, 4 * t), refs[-2], copies, res)
    hand_out(counts, lambda i: i * PIECE, res, outs)


def early_kernel(own, up, down, *refs):
    copies = start_all(refs[:4], refs[-2], refs[-1])
    trio, res = refs[4:6]
    t = own.shape[1]
    for k, ref in enumerate((own, up, down)):
        trio[:, k * t:(k + 1) * t] = ref[...]
    gradient_terms(trio, slice(0, 3 * t), refs[-2], copies, res)


def late_kernel(counts, where, f0, f1, early, *refs):
    copies = start_all(refs[:4], refs[-2], refs[-1])
    trio, outs, res = refs[4], refs[5:-3], refs[-3]
    t = 2 * f0.shape[1]
    trio[:, : t // 2] = f0[...]
    trio[:, t // 2:] = f1[...]
    res[:, : 3 * t] = early[...]
    gradient_terms(trio, slice(3 * t, 4 * t), refs[-2], copies, res)
    hand_out(counts, lambda i: place_of(i, sum(counts) // 4, where[0]), res, outs)


def backward_call(kernel, name, smem, inputs, mine, other, rows, outs, scratch=()):
    d, f = mine[0].shape
    return pl.pallas_call(
        kernel,
        out_shape=outs,
        in_specs=[SMEM] * len(smem) + vmem(len(inputs)) + [pl.BlockSpec(memory_space=pltpu.HBM)] * 4,
        out_specs=tuple(vmem(len(outs))),
        scratch_shapes=[*scratch, pltpu.VMEM((4, d, f), BF), pltpu.SemaphoreType.DMA((4,))],
        compiler_params=params(28),
        cost_estimate=pl.CostEstimate(flops=8 * rows * d * f, bytes_accessed=8 * d * f + rows * (6 * f + 4 * d), transcendentals=0),
        name=name,
    )(*smem, *inputs, *mine[:2], *other[:2])


def backward(parts, mine, other, counts):
    d, f = mine[0].shape
    rows = sum(counts) * PIECE
    outs = shape(3, rows, f), *(shape(n, 2, PIECE, d) for n in counts)
    kernel = functools.partial(backward_kernel, counts)
    return backward_call(kernel, "backward", (), (parts,), mine, other, rows, outs, (pltpu.VMEM((2, rows, d), BF),))


def backward_early(own, up, down, mine, other):
    d, f = mine[0].shape
    rows = 3 * own.shape[1]
    return backward_call(early_kernel, "backward_early", (), (own, up, down), mine, other, rows, (shape(3, rows, f), shape(2, rows, d)))


def backward_late(where, f0, f1, early, mine, other, counts):
    d, f = mine[0].shape
    t = 2 * f0.shape[1]
    outs = shape(3, t, f), *(shape(n, 2, PIECE, d) for n in counts)
    kernel = functools.partial(late_kernel, counts)
    return backward_call(kernel, "backward_late", (where,), (f0, f1, early), mine, other, t, outs, (pltpu.VMEM((2, 4 * t, d), BF),))


def weights_kernel(n, m, *refs):
    rows, trios = refs[:n], refs[n:n + m]
    o_gate, o_up, x, both = refs[n + m:]
    f = o_gate.shape[1]

    @pl.when(pl.program_id(0) == 0)
    def _():
        at = 0
        for ref in trios:
            k = ref.shape[1]
            both[at:at + k, :f] = ref[0]
            both[at:at + k, f:] = ref[1]
            at += k

    at = 0
    for ref in rows:
        k = ref.shape[1]
        x[at:at + k, :] = ref[0]
        at += k
    value = lax.dot_general(x[...], both[...], ROWS, preferred_element_type=F32).astype(BF)
    o_gate[...] = value[:, :f]
    o_up[...] = value[:, f:]


def weights(rows, trios):
    n = len(rows)
    d, f = rows[0].shape[2], trios[0].shape[2]
    tokens = sum(t.shape[1] for t in trios)
    w = 512
    return pl.pallas_call(
        functools.partial(weights_kernel, n, len(trios)),
        grid=(d // w,),
        out_shape=(shape(d, f), shape(d, f)),
        in_specs=[pl.BlockSpec((1, r.shape[1], w), lambda i: (0, 0, i)) for r in rows]
        + [pl.BlockSpec((pl.Element(2, (0, 0)), pl.Element(t.shape[1]), pl.Element(f)), lambda i: (1, 0, 0)) for t in trios],
        out_specs=[pl.BlockSpec((w, f), lambda i: (i, 0))] * 2,
        scratch_shapes=[pltpu.VMEM((tokens, w), BF), pltpu.VMEM((tokens, 2 * f), BF)],
        compiler_params=params(32),
        cost_estimate=pl.CostEstimate(flops=4 * tokens * d * f, bytes_accessed=4 * d * f + tokens * (2 * d + 4 * f), transcendentals=0),
        name="weights",
    )(*rows, *trios)


def down_kernel(n, m, *refs):
    rows, trios = refs[:n], refs[n:n + m]
    o_down, y, turned = refs[n + m:]

    @pl.when(pl.program_id(0) == 0)
    def _():
        at = 0
        for ref in trios:
            k = ref.shape[1]
            turned[:, at:at + k] = ref[0].T
            at += k

    at = 0
    for ref in rows:
        k = ref.shape[1]
        y[at:at + k, :] = ref[0]
        at += k
    o_down[...] = jnp.dot(turned[...], y[...], preferred_element_type=F32).astype(BF)


def down_weights(rows, trios):
    n = len(rows)
    d, f = rows[0].shape[2], trios[0].shape[2]
    tokens = sum(t.shape[1] for t in trios)
    w = 512
    return pl.pallas_call(
        functools.partial(down_kernel, n, len(trios)),
        grid=(d // w,),
        out_shape=shape(f, d),
        in_specs=[pl.BlockSpec((1, r.shape[1], w), lambda i: (1, 0, i)) for r in rows]
        + [pl.BlockSpec((1, t.shape[1], f), lambda i: (0, 0, 0)) for t in trios],
        out_specs=pl.BlockSpec((f, w), lambda i: (0, i)),
        scratch_shapes=[pltpu.VMEM((tokens, w), BF), pltpu.VMEM((f, tokens), BF)],
        compiler_params=params(32),
        cost_estimate=pl.CostEstimate(flops=2 * tokens * d * f, bytes_accessed=2 * d * f + tokens * (2 * d + 2 * f), transcendentals=0),
        name="down_weights",
    )(*rows, *trios)


def plus(a, *rest):
    total = a.astype(F32)
    for b in rest:
        total = total + b.astype(F32)
    return total


def after(value, *others):
    return lax.optimization_barrier((value, others))[0]


def to_all_z(value):
    return lax.all_to_all(value, "inp", 0, 0, axis_index_groups=[[0, 2, 4, 6], [1, 3, 5, 7]])


def local(tokens_in, grad_out, w_gate, w_up, w_down):
    inp = lax.axis_index("inp")
    core = inp % 2
    where = jnp.stack([inp // 2]).astype(jnp.int32)
    mine = (w_gate, w_up, w_down)

    own = jnp.stack([tokens_in, grad_out])
    kept = lax.dynamic_slice_in_dim(own, core * PIECE, PIECE, axis=1)
    given = lax.dynamic_slice_in_dim(own, (1 - core) * PIECE, PIECE, axis=1)
    piece = jnp.stack([kept, from_core(given)])
    line = jnp.stack([piece] + [from_line(piece, o) for o in OFFSETS[1:]])
    other = tuple(from_core(w) for w in after(mine, line))
    ahead, behind = from_side(line, 1), from_side(line, -1)
    far = from_side(ahead[:2], 1), from_side(behind[2:], -1)

    near_pieces = (line, ahead, behind)
    near_mine, near_other, b0, b1, b2, h0, h1 = forward(where, near_pieces, mine, other, True)
    r0, r1 = from_z(h0, -1), from_z(h1, 1)
    far_mine, far_other, parts = forward(where, far, mine, other, False)
    r0, r1 = after((r0, r1), parts)
    sums_far = to_all_z(parts)
    b1, b2 = add_far(b1, b2, r0, r1)
    q1, q2 = from_z(b1, -1), from_z(b2, 1)
    near_got, far_got = from_core(near_other), from_core(far_other)
    trio_far = activate(sums_far)
    q1, q2 = after((q1, q2), trio_far)
    trio = activate(b0, q1, q2)
    t = trio.shape[1]
    up, down = from_z(trio, 1), from_z(trio, -1)
    trio_far, far0, far1 = backward(to_all_z(trio_far), mine, other, (2, 2))
    up, down = after((up, down), (far0, far1))
    far0, far1 = from_side(far0, -1), from_side(far1, 1)
    f0, f1 = from_z(down[:, : t // 2], -1), from_z(up[:, t // 2:], 1)
    trio_early, early = backward_early(trio, up, down, mine, other)
    f0, f1 = after((f0, f1), (far0, far1, early))
    trio_far_got, trio_early_got = (from_core(v) for v in after((trio_far, trio_early), f0))
    trio_late, line, ahead, behind = backward_late(where, f0, f1, early, mine, other, (4, 4, 4))
    trio_late_got = from_core(trio_late)

    ahead = jnp.concatenate([plus(ahead[:2], far0).astype(BF), ahead[2:]])
    behind = jnp.concatenate([behind[:2], plus(behind[2:], far1).astype(BF)])
    ahead, behind = from_side(ahead, -1), from_side(behind, 1)

    rows = near_mine, far_mine, near_got, far_got
    trios = trio_early, trio_late, trio_far, trio_early_got, trio_late_got, trio_far_got
    gate_up = weights(rows, trios)
    ahead, behind = after((ahead, behind), gate_up)

    line = plus(line, ahead, behind)
    sent = [from_line(line[j].astype(BF), -OFFSETS[j]) for j in range(1, 4)]
    grad_w_down = down_weights(rows, trios)
    sent = after(sent, grad_w_down)
    sums = plus(line[0], *sent).astype(BF)
    got = from_core(sums[1])
    first = core == 0
    grad_tokens = jnp.concatenate([jnp.where(first, sums[0], got), jnp.where(first, got, sums[0])])
    return (grad_tokens, *gate_up, grad_w_down)


def solution(mesh):
    return jax.shard_map(
        local,
        mesh=mesh,
        in_specs=(P(XY, "inp"), P(XY, "inp"), P("inp", XY), P("inp", XY), P(XY, "inp")),
        out_specs=(P(XY, "inp"), P("inp", XY), P("inp", XY), P(XY, "inp")),
        check_vma=False,
    )
```

```python
import functools

import jax
import jax.numpy as jnp
from jax import lax
from jax.experimental import pallas as pl
from jax.experimental.pallas import tpu as pltpu
from jax.sharding import PartitionSpec as P

XY = ("out", "dep")
ALL = ("inp", "out", "dep")
BF = jnp.bfloat16
F32 = jnp.float32
MB = 1024 * 1024
PIECE = 32
OFFSETS = (0, 1, 3, 2)
ROWS = (((0,), (0,)), ((), ()))
LANES = (((1,), (1,)), ((), ()))


def index(x, y, z, c):
    return (z * 2 + c) * 16 + ((y % 2) * 4 + x) * 2 + y // 2


def from_where(value, shift):
    pairs = []
    for x in range(4):
        for y in range(4):
            for z in range(4):
                for c in range(2):
                    a, b, d, e = shift(x, y, z, c)
                    pairs.append((index(a % 4, b % 4, d % 4, e % 2), index(x, y, z, c)))
    return lax.ppermute(value, ALL, pairs)


def from_line(value, step):
    return from_where(value, lambda x, y, z, c: (x + (step if c == 0 else 0), y + (step if c == 1 else 0), z, c))


def from_side(value, step):
    return from_where(value, lambda x, y, z, c: (x + (step if c == 1 else 0), y + (step if c == 0 else 0), z, c))


def from_z(value, step):
    return from_where(value, lambda x, y, z, c: (x, y, z + step, c))


def from_core(value):
    return from_where(value, lambda x, y, z, c: (x, y, z, c + 1))


def params(mb=48):
    return pltpu.CompilerParams(vmem_limit_bytes=mb * MB)


def vmem(n):
    return [pl.BlockSpec(memory_space=pltpu.VMEM)] * n


def shape(*dims, dtype=BF):
    return jax.ShapeDtypeStruct(dims, dtype)


def hbm(arrays):
    return [pltpu.with_memory_space_constraint(a, pltpu.HBM) for a in arrays]


SMEM = pl.BlockSpec(memory_space=pltpu.SMEM)


def place_of(i, per, z):
    if z is None:
        return i * PIECE
    away = lax.rem(i // per - z + 4, 4)
    away = jnp.where(away == 3, 2, jnp.where(away == 2, 3, away))
    return pl.multiple_of((away * per + i % per) * PIECE, PIECE)


def forward_kernel(counts, ring, where, *refs):
    n = len(counts)
    pieces, mine, other = refs[:n], refs[n:n + 3], refs[n + 3:n + 6]
    rows_mine, rows_other, *outs, rows, wide, down, sems = refs[n + 6:]
    held = wide.at[0], wide.at[1], wide.at[2], wide.at[3], down.at[0], down.at[1]
    per = sum(counts) // 4
    t = per * PIECE
    moves = []
    for ref, count in zip(pieces, counts):
        for j in range(count):
            row = place_of(len(moves), per, where[0] if ring else None)
            moves.append((ref.at[j], rows.at[:, :, pl.ds(row, PIECE), :]))
    total = len(moves)
    moves += list(zip((mine[0], other[0], mine[1], other[1], mine[2], other[2]), held))
    copies = [pltpu.make_async_copy(a, b, sems.at[k]) for k, (a, b) in enumerate(moves)]
    for copy in copies:
        copy.start()
    for copy in copies[:total]:
        copy.wait()
    copies = copies[total:]
    results = [pltpu.make_async_copy(rows.at[k], out, sems.at[k]) for k, out in enumerate((rows_mine, rows_other))]
    for m in range(3):
        src = 0 if m < 2 else 1
        dims = (((1,), (0,)), ((), ())) if m < 2 else LANES
        copies[2 * m].wait()
        v = lax.dot_general(rows[0, src], held[2 * m][...], dims, preferred_element_type=F32)
        copies[2 * m + 1].wait()
        if m == 2:
            for copy in results:
                copy.start()
        v = v + lax.dot_general(rows[1, src], held[2 * m + 1][...], dims, preferred_element_type=F32)
        v = v.astype(BF)
        for block in range(4):
            part = v[block * t:(block + 1) * t]
            if not ring:
                outs[0][block, m] = part
            elif block < 3:
                outs[block][m] = part
            else:
                outs[3][m] = part[: t // 2]
                outs[4][m] = part[t // 2:]
    for copy in results:
        copy.wait()


def forward(where, pieces, mine, other, ring):
    counts = tuple(p.shape[0] for p in pieces)
    t = sum(counts) // 4 * PIECE
    d, f = mine[0].shape
    rows = pltpu.HBM((2, 4 * t, d), BF)
    whole, half = shape(3, t, f), shape(3, t // 2, f)
    outs = (whole, whole, whole, half, half) if ring else (shape(4, 3, t, f),)
    far = [pl.BlockSpec(memory_space=pltpu.HBM)]
    return pl.pallas_call(
        functools.partial(forward_kernel, counts, ring),
        out_shape=(rows, rows, *outs),
        in_specs=[SMEM] + far * (len(pieces) + 6),
        out_specs=far * 2 + vmem(len(outs)),
        scratch_shapes=[
            pltpu.VMEM((2, 2, 4 * t, d), BF),
            pltpu.VMEM((4, d, f), BF),
            pltpu.VMEM((2, f, d), BF),
            pltpu.SemaphoreType.DMA((sum(counts) + 6,)),
        ],
        compiler_params=params(18 + 16 * t // 256),
        cost_estimate=pl.CostEstimate(flops=12 * 4 * t * d * f, bytes_accessed=12 * d * f + 64 * t * d, transcendentals=0),
        name="forward",
    )(where, *hbm(pieces), *hbm(mine), *hbm(other))


def add_far_kernel(b1, b2, r0, r1, o1, o2):
    t = b1.shape[1]
    o1[:, : t // 2] = (b1[:, : t // 2].astype(F32) + r0[...].astype(F32)).astype(BF)
    o1[:, t // 2:] = b1[:, t // 2:]
    o2[:, : t // 2] = b2[:, : t // 2]
    o2[:, t // 2:] = (b2[:, t // 2:].astype(F32) + r1[...].astype(F32)).astype(BF)


def add_far(b1, b2, r0, r1):
    return pl.pallas_call(
        add_far_kernel,
        out_shape=(shape(*b1.shape), shape(*b1.shape)),
        in_specs=vmem(4),
        out_specs=vmem(2),
        compiler_params=params(8),
        name="add_far",
    )(b1, b2, r0, r1)


def activate_kernel(n, *refs):
    parts, outs = refs[:n], refs[n:]

    def total(m):
        if n == 1:
            return sum(parts[0][k, m].astype(F32) for k in range(4))
        return sum(p[m].astype(F32) for p in parts)

    gate, up, back = (total(m) for m in range(3))
    sig = 1.0 / (1.0 + jnp.exp(-gate))
    silu = gate * sig
    values = (silu * up, back * up * sig * (1.0 + gate * (1.0 - sig)), back * silu)
    for m, v in enumerate(values):
        v = v.astype(BF)
        if n == 1:
            for k in range(4):
                outs[0][k, m] = v
        else:
            outs[0][m] = v


def activate(*parts):
    return pl.pallas_call(
        functools.partial(activate_kernel, len(parts)),
        out_shape=shape(*parts[0].shape),
        in_specs=vmem(len(parts)),
        out_specs=vmem(1)[0],
        compiler_params=params(8),
        name="activate",
    )(*parts)


def gradient_terms(trio, rows, held, copies, res):
    for b in range(2):
        copies[2 * b].wait()
        v = lax.dot_general(trio[1], held[2 * b], LANES, preferred_element_type=F32)
        copies[2 * b + 1].wait()
        v = v + lax.dot_general(trio[2], held[2 * b + 1], LANES, preferred_element_type=F32)
        res[b, rows] = v.astype(BF)


def start_all(sources, targets, sems):
    copies = [pltpu.make_async_copy(a, targets.at[k], sems.at[k]) for k, a in enumerate(sources)]
    for copy in copies:
        copy.start()
    return copies


def hand_out(counts, place, res, outs):
    i = 0
    for ref, count in zip(outs, counts):
        for j in range(count):
            row = place(i)
            for b in range(2):
                ref[j, b] = res[b, pl.ds(row, PIECE), :]
            i += 1


def backward_kernel(counts, parts, *refs):
    copies = start_all(refs[:4], refs[-2], refs[-1])
    trio, outs, res = refs[4], refs[5:-3], refs[-3]
    t = parts.shape[2]
    for k in range(4):
        for m in range(3):
            trio[m, k * t:(k + 1) * t] = parts[k, m]
    gradient_terms(trio, slice(0, 4 * t), refs[-2], copies, res)
    hand_out(counts, lambda i: i * PIECE, res, outs)


def early_kernel(own, up, down, *refs):
    copies = start_all(refs[:4], refs[-2], refs[-1])
    trio, res = refs[4:6]
    t = own.shape[1]
    for k, ref in enumerate((own, up, down)):
        trio[:, k * t:(k + 1) * t] = ref[...]
    gradient_terms(trio, slice(0, 3 * t), refs[-2], copies, res)


def late_kernel(counts, where, f0, f1, early, far0, far1, *refs):
    copies = start_all(refs[:4], refs[-2], refs[-1])
    trio, outs, res = refs[4], refs[5:-3], refs[-3]
    t = 2 * f0.shape[1]
    trio[:, : t // 2] = f0[...]
    trio[:, t // 2:] = f1[...]
    res[:, : 3 * t] = early[...]
    gradient_terms(trio, slice(3 * t, 4 * t), refs[-2], copies, res)
    hand_out(counts, lambda i: place_of(i, sum(counts) // 4, where[0]), res, outs)
    for ref, first, got in ((outs[1], 0, far0), (outs[2], 2, far1)):
        for j in range(2):
            ref[first + j] = (ref[first + j].astype(F32) + got[j].astype(F32)).astype(BF)


def backward_call(kernel, name, smem, inputs, mine, other, rows, outs, scratch=()):
    d, f = mine[0].shape
    return pl.pallas_call(
        kernel,
        out_shape=outs,
        in_specs=[SMEM] * len(smem) + vmem(len(inputs)) + [pl.BlockSpec(memory_space=pltpu.HBM)] * 4,
        out_specs=tuple(vmem(len(outs))),
        scratch_shapes=[*scratch, pltpu.VMEM((4, d, f), BF), pltpu.SemaphoreType.DMA((4,))],
        compiler_params=params(28),
        cost_estimate=pl.CostEstimate(flops=8 * rows * d * f, bytes_accessed=8 * d * f + rows * (6 * f + 4 * d), transcendentals=0),
        name=name,
    )(*smem, *inputs, *mine[:2], *other[:2])


def backward(parts, mine, other, counts):
    d, f = mine[0].shape
    rows = sum(counts) * PIECE
    outs = shape(3, rows, f), *(shape(n, 2, PIECE, d) for n in counts)
    kernel = functools.partial(backward_kernel, counts)
    return backward_call(kernel, "backward", (), (parts,), mine, other, rows, outs, (pltpu.VMEM((2, rows, d), BF),))


def backward_early(own, up, down, mine, other):
    d, f = mine[0].shape
    rows = 3 * own.shape[1]
    return backward_call(early_kernel, "backward_early", (), (own, up, down), mine, other, rows, (shape(3, rows, f), shape(2, rows, d)))


def backward_late(where, f0, f1, early, far0, far1, mine, other, counts):
    d, f = mine[0].shape
    t = 2 * f0.shape[1]
    outs = shape(3, t, f), *(shape(n, 2, PIECE, d) for n in counts)
    kernel = functools.partial(late_kernel, counts)
    return backward_call(kernel, "backward_late", (where,), (f0, f1, early, far0, far1), mine, other, t, outs, (pltpu.VMEM((2, 4 * t, d), BF),))


def weights_kernel(n, m, *refs):
    rows, trios = refs[:n], refs[n:n + m]
    o_gate, o_up, x, both = refs[n + m:]
    f = o_gate.shape[1]

    @pl.when(pl.program_id(0) == 0)
    def _():
        at = 0
        for ref in trios:
            k = ref.shape[1]
            both[at:at + k, :f] = ref[0]
            both[at:at + k, f:] = ref[1]
            at += k

    at = 0
    for ref in rows:
        k = ref.shape[1]
        x[at:at + k, :] = ref[0]
        at += k
    value = lax.dot_general(x[...], both[...], ROWS, preferred_element_type=F32).astype(BF)
    o_gate[...] = value[:, :f]
    o_up[...] = value[:, f:]


def weights(rows, trios):
    n = len(rows)
    d, f = rows[0].shape[2], trios[0].shape[2]
    tokens = sum(t.shape[1] for t in trios)
    w = 512
    return pl.pallas_call(
        functools.partial(weights_kernel, n, len(trios)),
        grid=(d // w,),
        out_shape=(shape(d, f), shape(d, f)),
        in_specs=[pl.BlockSpec((1, r.shape[1], w), lambda i: (0, 0, i)) for r in rows]
        + [pl.BlockSpec((pl.Element(2, (0, 0)), pl.Element(t.shape[1]), pl.Element(f)), lambda i: (1, 0, 0)) for t in trios],
        out_specs=[pl.BlockSpec((w, f), lambda i: (i, 0))] * 2,
        scratch_shapes=[pltpu.VMEM((tokens, w), BF), pltpu.VMEM((tokens, 2 * f), BF)],
        compiler_params=params(32),
        cost_estimate=pl.CostEstimate(flops=4 * tokens * d * f, bytes_accessed=4 * d * f + tokens * (2 * d + 4 * f), transcendentals=0),
        name="weights",
    )(*rows, *trios)


def down_kernel(n, m, *refs):
    rows, trios = refs[:n], refs[n:n + m]
    o_down, y, turned = refs[n + m:]

    @pl.when(pl.program_id(0) == 0)
    def _():
        at = 0
        for ref in trios:
            k = ref.shape[1]
            turned[:, at:at + k] = ref[0].T
            at += k

    at = 0
    for ref in rows:
        k = ref.shape[1]
        y[at:at + k, :] = ref[0]
        at += k
    o_down[...] = jnp.dot(turned[...], y[...], preferred_element_type=F32).astype(BF)


def down_weights(rows, trios):
    n = len(rows)
    d, f = rows[0].shape[2], trios[0].shape[2]
    tokens = sum(t.shape[1] for t in trios)
    w = 512
    return pl.pallas_call(
        functools.partial(down_kernel, n, len(trios)),
        grid=(d // w,),
        out_shape=shape(f, d),
        in_specs=[pl.BlockSpec((1, r.shape[1], w), lambda i: (1, 0, i)) for r in rows]
        + [pl.BlockSpec((1, t.shape[1], f), lambda i: (0, 0, 0)) for t in trios],
        out_specs=pl.BlockSpec((f, w), lambda i: (0, i)),
        scratch_shapes=[pltpu.VMEM((tokens, w), BF), pltpu.VMEM((f, tokens), BF)],
        compiler_params=params(32),
        cost_estimate=pl.CostEstimate(flops=2 * tokens * d * f, bytes_accessed=2 * d * f + tokens * (2 * d + 2 * f), transcendentals=0),
        name="down_weights",
    )(*rows, *trios)


def plus(a, *rest):
    total = a.astype(F32)
    for b in rest:
        total = total + b.astype(F32)
    return total


def after(value, *others):
    return lax.optimization_barrier((value, others))[0]


def to_all_z(value):
    return lax.all_to_all(value, "inp", 0, 0, axis_index_groups=[[0, 2, 4, 6], [1, 3, 5, 7]])


def local(tokens_in, grad_out, w_gate, w_up, w_down):
    inp = lax.axis_index("inp")
    core = inp % 2
    where = jnp.stack([inp // 2]).astype(jnp.int32)
    mine = (w_gate, w_up, w_down)

    own = jnp.stack([tokens_in, grad_out])
    kept = lax.dynamic_slice_in_dim(own, core * PIECE, PIECE, axis=1)
    given = lax.dynamic_slice_in_dim(own, (1 - core) * PIECE, PIECE, axis=1)
    piece = jnp.stack([kept, from_core(given)])
    line = jnp.stack([piece] + [from_line(piece, o) for o in OFFSETS[1:]])
    other = tuple(from_core(w) for w in after(mine, line))
    ahead, behind = from_side(line, 1), from_side(line, -1)
    far = from_side(ahead[:2], 1), from_side(behind[2:], -1)

    near_pieces = (line, ahead, behind)
    near_mine, near_other, b0, b1, b2, h0, h1 = forward(where, near_pieces, mine, other, True)
    r0, r1 = from_z(h0, -1), from_z(h1, 1)
    far_mine, far_other, parts = forward(where, far, mine, other, False)
    r0, r1 = after((r0, r1), parts)
    sums_far = to_all_z(parts)
    b1, b2 = add_far(b1, b2, r0, r1)
    q1, q2 = from_z(b1, -1), from_z(b2, 1)
    near_got, far_got = from_core(near_other), from_core(far_other)
    trio_far = activate(sums_far)
    q1, q2 = after((q1, q2), trio_far)
    trio = activate(b0, q1, q2)
    t = trio.shape[1]
    up, down = from_z(trio, 1), from_z(trio, -1)
    trio_far, far0, far1 = backward(to_all_z(trio_far), mine, other, (2, 2))
    up, down = after((up, down), (far0, far1))
    far0, far1 = from_side(far0, -1), from_side(far1, 1)
    f0, f1 = from_z(down[:, : t // 2], -1), from_z(up[:, t // 2:], 1)
    trio_early, early = backward_early(trio, up, down, mine, other)
    f0, f1 = after((f0, f1), (far0, far1, early))
    trio_far_got, trio_early_got = (from_core(v) for v in after((trio_far, trio_early), f0))
    trio_late, line, ahead, behind = backward_late(where, f0, f1, early, far0, far1, mine, other, (4, 4, 4))
    trio_late_got = from_core(trio_late)

    ahead, behind = from_side(ahead, -1), from_side(behind, 1)

    rows = near_mine, far_mine, near_got, far_got
    trios = trio_early, trio_late, trio_far, trio_early_got, trio_late_got, trio_far_got
    gate_up = weights(rows, trios)
    ahead, behind = after((ahead, behind), gate_up)

    line = plus(line, ahead, behind)
    sent = [from_line(line[j].astype(BF), -OFFSETS[j]) for j in range(1, 4)]
    grad_w_down = down_weights(rows, trios)
    sent = after(sent, grad_w_down)
    sums = plus(line[0], *sent).astype(BF)
    got = from_core(sums[1])
    first = core == 0
    grad_tokens = jnp.concatenate([jnp.where(first, sums[0], got), jnp.where(first, got, sums[0])])
    return (grad_tokens, *gate_up, grad_w_down)


def solution(mesh):
    return jax.shard_map(
        local,
        mesh=mesh,
        in_specs=(P(XY, "inp"), P(XY, "inp"), P("inp", XY), P("inp", XY), P(XY, "inp")),
        out_specs=(P(XY, "inp"), P("inp", XY), P("inp", XY), P(XY, "inp")),
        check_vma=False,
    )
```

```python
import functools

import jax
import jax.numpy as jnp
from jax import lax
from jax.experimental import pallas as pl
from jax.experimental.pallas import tpu as pltpu
from jax.sharding import PartitionSpec as P

XY = ("out", "dep")
ALL = ("inp", "out", "dep")
BF = jnp.bfloat16
F32 = jnp.float32
MB = 1024 * 1024
PIECE = 32
OFFSETS = (0, 1, 3, 2)
ROWS = (((0,), (0,)), ((), ()))
LANES = (((1,), (1,)), ((), ()))


def index(x, y, z, c):
    return (z * 2 + c) * 16 + ((y % 2) * 4 + x) * 2 + y // 2


def from_where(value, shift):
    pairs = []
    for x in range(4):
        for y in range(4):
            for z in range(4):
                for c in range(2):
                    a, b, d, e = shift(x, y, z, c)
                    pairs.append((index(a % 4, b % 4, d % 4, e % 2), index(x, y, z, c)))
    return lax.ppermute(value, ALL, pairs)


def from_line(value, step):
    return from_where(value, lambda x, y, z, c: (x + (step if c == 0 else 0), y + (step if c == 1 else 0), z, c))


def from_side(value, step):
    return from_where(value, lambda x, y, z, c: (x + (step if c == 1 else 0), y + (step if c == 0 else 0), z, c))


def from_z(value, step):
    return from_where(value, lambda x, y, z, c: (x, y, z + step, c))


def from_core(value):
    return from_where(value, lambda x, y, z, c: (x, y, z, c + 1))


def params(mb=48):
    return pltpu.CompilerParams(vmem_limit_bytes=mb * MB)


def vmem(n):
    return [pl.BlockSpec(memory_space=pltpu.VMEM)] * n


def shape(*dims, dtype=BF):
    return jax.ShapeDtypeStruct(dims, dtype)


def hbm(arrays):
    return [pltpu.with_memory_space_constraint(a, pltpu.HBM) for a in arrays]


SMEM = pl.BlockSpec(memory_space=pltpu.SMEM)


def place_of(i, per, z):
    if z is None:
        return i * PIECE
    away = lax.rem(i // per - z + 4, 4)
    away = jnp.where(away == 3, 2, jnp.where(away == 2, 3, away))
    return pl.multiple_of((away * per + i % per) * PIECE, PIECE)


def forward_kernel(counts, ring, where, *refs):
    n = len(counts)
    pieces, mine, other = refs[:n], refs[n:n + 3], refs[n + 3:n + 6]
    rows_mine, rows_other, *outs, rows, wide, down, sems = refs[n + 6:]
    held = wide.at[0], wide.at[1], wide.at[2], wide.at[3], down.at[0], down.at[1]
    per = sum(counts) // 4
    t = per * PIECE
    moves = []
    for ref, count in zip(pieces, counts):
        for j in range(count):
            row = place_of(len(moves), per, where[0] if ring else None)
            moves.append((ref.at[j], rows.at[:, :, pl.ds(row, PIECE), :]))
    total = len(moves)
    moves += list(zip((mine[0], other[0], mine[1], other[1], mine[2], other[2]), held))
    copies = [pltpu.make_async_copy(a, b, sems.at[k]) for k, (a, b) in enumerate(moves)]
    for copy in copies:
        copy.start()
    for copy in copies[:total]:
        copy.wait()
    copies = copies[total:]
    results = [pltpu.make_async_copy(rows.at[k], out, sems.at[k]) for k, out in enumerate((rows_mine, rows_other))]
    for m in range(3):
        src = 0 if m < 2 else 1
        dims = (((1,), (0,)), ((), ())) if m < 2 else LANES
        copies[2 * m].wait()
        v = lax.dot_general(rows[0, src], held[2 * m][...], dims, preferred_element_type=F32)
        copies[2 * m + 1].wait()
        if m == 2:
            for copy in results:
                copy.start()
        v = v + lax.dot_general(rows[1, src], held[2 * m + 1][...], dims, preferred_element_type=F32)
        v = v.astype(BF)
        for block in range(4):
            part = v[block * t:(block + 1) * t]
            if not ring:
                outs[0][block, m] = part
            elif block < 3:
                outs[block][m] = part
            else:
                outs[3][m] = part[: t // 2]
                outs[4][m] = part[t // 2:]
    for copy in results:
        copy.wait()


def forward(where, pieces, mine, other, ring):
    counts = tuple(p.shape[0] for p in pieces)
    t = sum(counts) // 4 * PIECE
    d, f = mine[0].shape
    rows = pltpu.HBM((2, 4 * t, d), BF)
    whole, half = shape(3, t, f), shape(3, t // 2, f)
    outs = (whole, whole, whole, half, half) if ring else (shape(4, 3, t, f),)
    far = [pl.BlockSpec(memory_space=pltpu.HBM)]
    return pl.pallas_call(
        functools.partial(forward_kernel, counts, ring),
        out_shape=(rows, rows, *outs),
        in_specs=[SMEM] + far * (len(pieces) + 6),
        out_specs=far * 2 + vmem(len(outs)),
        scratch_shapes=[
            pltpu.VMEM((2, 2, 4 * t, d), BF),
            pltpu.VMEM((4, d, f), BF),
            pltpu.VMEM((2, f, d), BF),
            pltpu.SemaphoreType.DMA((sum(counts) + 6,)),
        ],
        compiler_params=params(18 + 16 * t // 256),
        cost_estimate=pl.CostEstimate(flops=12 * 4 * t * d * f, bytes_accessed=12 * d * f + 64 * t * d, transcendentals=0),
        name="forward",
    )(where, *hbm(pieces), *hbm(mine), *hbm(other))


def add_far_kernel(b1, b2, r0, r1, o1, o2):
    t = b1.shape[1]
    o1[:, : t // 2] = (b1[:, : t // 2].astype(F32) + r0[...].astype(F32)).astype(BF)
    o1[:, t // 2:] = b1[:, t // 2:]
    o2[:, : t // 2] = b2[:, : t // 2]
    o2[:, t // 2:] = (b2[:, t // 2:].astype(F32) + r1[...].astype(F32)).astype(BF)


def add_far(b1, b2, r0, r1):
    return pl.pallas_call(
        add_far_kernel,
        out_shape=(shape(*b1.shape), shape(*b1.shape)),
        in_specs=vmem(4),
        out_specs=vmem(2),
        compiler_params=params(8),
        name="add_far",
    )(b1, b2, r0, r1)


def activate_kernel(n, *refs):
    parts, outs = refs[:n], refs[n:]

    def total(m):
        if n == 1:
            return sum(parts[0][k, m].astype(F32) for k in range(4))
        return sum(p[m].astype(F32) for p in parts)

    gate, up, back = (total(m) for m in range(3))
    sig = 1.0 / (1.0 + jnp.exp(-gate))
    silu = gate * sig
    values = (silu * up, back * up * sig * (1.0 + gate * (1.0 - sig)), back * silu)
    for m, v in enumerate(values):
        v = v.astype(BF)
        if n == 1:
            for k in range(4):
                outs[0][k, m] = v
        else:
            outs[0][m] = v


def activate(*parts):
    return pl.pallas_call(
        functools.partial(activate_kernel, len(parts)),
        out_shape=shape(*parts[0].shape),
        in_specs=vmem(len(parts)),
        out_specs=vmem(1)[0],
        compiler_params=params(8),
        name="activate",
    )(*parts)


def gradient_terms(trio, rows, held, copies, res):
    for b in range(2):
        copies[2 * b].wait()
        v = lax.dot_general(trio[1], held[2 * b], LANES, preferred_element_type=F32)
        copies[2 * b + 1].wait()
        v = v + lax.dot_general(trio[2], held[2 * b + 1], LANES, preferred_element_type=F32)
        res[b, rows] = v.astype(BF)


def start_all(sources, targets, sems):
    copies = [pltpu.make_async_copy(a, targets.at[k], sems.at[k]) for k, a in enumerate(sources)]
    for copy in copies:
        copy.start()
    return copies


def hand_out(counts, place, res, outs):
    i = 0
    for ref, count in zip(outs, counts):
        for j in range(count):
            row = place(i)
            for b in range(2):
                ref[j, b] = res[b, pl.ds(row, PIECE), :]
            i += 1


def backward_kernel(counts, parts, *refs):
    copies = start_all(refs[:4], refs[-2], refs[-1])
    trio, outs, res = refs[4], refs[5:-3], refs[-3]
    t = parts.shape[2]
    for k in range(4):
        for m in range(3):
            trio[m, k * t:(k + 1) * t] = parts[k, m]
    gradient_terms(trio, slice(0, 4 * t), refs[-2], copies, res)
    hand_out(counts, lambda i: i * PIECE, res, outs)


def early_kernel(own, up, down, *refs):
    copies = start_all(refs[:4], refs[-2], refs[-1])
    trio, res = refs[4:6]
    t = own.shape[1]
    for k, ref in enumerate((own, up, down)):
        trio[:, k * t:(k + 1) * t] = ref[...]
    gradient_terms(trio, slice(0, 3 * t), refs[-2], copies, res)


def late_kernel(counts, where, f0, f1, early, far0, far1, *refs):
    copies = start_all(refs[:4], refs[-2], refs[-1])
    trio, outs, res = refs[4], refs[5:-3], refs[-3]
    t = 2 * f0.shape[1]
    trio[:, : t // 2] = f0[...]
    trio[:, t // 2:] = f1[...]
    res[:, : 3 * t] = early[...]
    gradient_terms(trio, slice(3 * t, 4 * t), refs[-2], copies, res)
    hand_out(counts, lambda i: place_of(i, sum(counts) // 4, where[0]), res, outs)
    for ref, first, got in ((outs[1], 0, far0), (outs[2], 2, far1)):
        for j in range(2):
            ref[first + j] = (ref[first + j].astype(F32) + got[j].astype(F32)).astype(BF)


def backward_call(kernel, name, smem, inputs, mine, other, rows, outs, scratch=()):
    d, f = mine[0].shape
    return pl.pallas_call(
        kernel,
        out_shape=outs,
        in_specs=[SMEM] * len(smem) + vmem(len(inputs)) + [pl.BlockSpec(memory_space=pltpu.HBM)] * 4,
        out_specs=tuple(vmem(len(outs))),
        scratch_shapes=[*scratch, pltpu.VMEM((4, d, f), BF), pltpu.SemaphoreType.DMA((4,))],
        compiler_params=params(28),
        cost_estimate=pl.CostEstimate(flops=8 * rows * d * f, bytes_accessed=8 * d * f + rows * (6 * f + 4 * d), transcendentals=0),
        name=name,
    )(*smem, *inputs, *mine[:2], *other[:2])


def backward(parts, mine, other, counts):
    d, f = mine[0].shape
    rows = sum(counts) * PIECE
    outs = shape(3, rows, f), *(shape(n, 2, PIECE, d) for n in counts)
    kernel = functools.partial(backward_kernel, counts)
    return backward_call(kernel, "backward", (), (parts,), mine, other, rows, outs, (pltpu.VMEM((2, rows, d), BF),))


def backward_early(own, up, down, mine, other):
    d, f = mine[0].shape
    rows = 3 * own.shape[1]
    return backward_call(early_kernel, "backward_early", (), (own, up, down), mine, other, rows, (shape(3, rows, f), shape(2, rows, d)))


def backward_late(where, f0, f1, early, far0, far1, mine, other, counts):
    d, f = mine[0].shape
    t = 2 * f0.shape[1]
    outs = shape(3, t, f), *(shape(n, 2, PIECE, d) for n in counts)
    kernel = functools.partial(late_kernel, counts)
    return backward_call(kernel, "backward_late", (where,), (f0, f1, early, far0, far1), mine, other, t, outs, (pltpu.VMEM((2, 4 * t, d), BF),))


def weights_kernel(n, m, *refs):
    rows, trios = refs[:n], refs[n:n + m]
    o_gate, o_up, x, both = refs[n + m:]
    f = o_gate.shape[1]

    @pl.when(pl.program_id(0) == 0)
    def _():
        at = 0
        for ref in trios:
            k = ref.shape[1]
            both[at:at + k, :f] = ref[0]
            both[at:at + k, f:] = ref[1]
            at += k

    at = 0
    for ref in rows:
        k = ref.shape[1]
        x[at:at + k, :] = ref[0]
        at += k
    value = lax.dot_general(x[...], both[...], ROWS, preferred_element_type=F32).astype(BF)
    o_gate[...] = value[:, :f]
    o_up[...] = value[:, f:]


def weights(rows, trios):
    n = len(rows)
    d, f = rows[0].shape[2], trios[0].shape[2]
    tokens = sum(t.shape[1] for t in trios)
    w = 512
    return pl.pallas_call(
        functools.partial(weights_kernel, n, len(trios)),
        grid=(d // w,),
        out_shape=(shape(d, f), shape(d, f)),
        in_specs=[pl.BlockSpec((1, r.shape[1], w), lambda i: (0, 0, i)) for r in rows]
        + [pl.BlockSpec((pl.Element(2, (0, 0)), pl.Element(t.shape[1]), pl.Element(f)), lambda i: (1, 0, 0)) for t in trios],
        out_specs=[pl.BlockSpec((w, f), lambda i: (i, 0))] * 2,
        scratch_shapes=[pltpu.VMEM((tokens, w), BF), pltpu.VMEM((tokens, 2 * f), BF)],
        compiler_params=params(32),
        cost_estimate=pl.CostEstimate(flops=4 * tokens * d * f, bytes_accessed=4 * d * f + tokens * (2 * d + 4 * f), transcendentals=0),
        name="weights",
    )(*rows, *trios)


def down_kernel(n, m, *refs):
    rows, trios = refs[:n], refs[n:n + m]
    o_down, y, turned = refs[n + m:]

    @pl.when(pl.program_id(0) == 0)
    def _():
        at = 0
        for ref in trios:
            k = ref.shape[1]
            turned[:, at:at + k] = ref[0].T
            at += k

    at = 0
    for ref in rows:
        k = ref.shape[1]
        y[at:at + k, :] = ref[0]
        at += k
    o_down[...] = jnp.dot(turned[...], y[...], preferred_element_type=F32).astype(BF)


def down_weights(rows, trios):
    n = len(rows)
    d, f = rows[0].shape[2], trios[0].shape[2]
    tokens = sum(t.shape[1] for t in trios)
    w = 512
    return pl.pallas_call(
        functools.partial(down_kernel, n, len(trios)),
        grid=(d // w,),
        out_shape=shape(f, d),
        in_specs=[pl.BlockSpec((1, r.shape[1], w), lambda i: (1, 0, i)) for r in rows]
        + [pl.BlockSpec((1, t.shape[1], f), lambda i: (0, 0, 0)) for t in trios],
        out_specs=pl.BlockSpec((f, w), lambda i: (0, i)),
        scratch_shapes=[pltpu.VMEM((tokens, w), BF), pltpu.VMEM((f, tokens), BF)],
        compiler_params=params(32),
        cost_estimate=pl.CostEstimate(flops=2 * tokens * d * f, bytes_accessed=2 * d * f + tokens * (2 * d + 2 * f), transcendentals=0),
        name="down_weights",
    )(*rows, *trios)


def plus(a, *rest):
    total = a.astype(F32)
    for b in rest:
        total = total + b.astype(F32)
    return total


def after(value, *others):
    return lax.optimization_barrier((value, others))[0]


def to_all_z(value):
    return lax.all_to_all(value, "inp", 0, 0, axis_index_groups=[[0, 2, 4, 6], [1, 3, 5, 7]])


def local(tokens_in, grad_out, w_gate, w_up, w_down):
    inp = lax.axis_index("inp")
    core = inp % 2
    where = jnp.stack([inp // 2]).astype(jnp.int32)
    mine = (w_gate, w_up, w_down)

    own = jnp.stack([tokens_in, grad_out])
    kept = lax.dynamic_slice_in_dim(own, core * PIECE, PIECE, axis=1)
    given = lax.dynamic_slice_in_dim(own, (1 - core) * PIECE, PIECE, axis=1)
    piece = jnp.stack([kept, from_core(given)])
    line = jnp.stack([piece] + [from_line(piece, o) for o in OFFSETS[1:]])
    other = tuple(from_core(w) for w in after(mine, line))
    ahead, behind = from_side(line, 1), from_side(line, -1)
    far = from_side(ahead[:2], 1), from_side(behind[2:], -1)

    near_pieces = (line, ahead, behind)
    near_mine, near_other, b0, b1, b2, h0, h1 = forward(where, near_pieces, mine, other, True)
    r0, r1 = from_z(h0, -1), from_z(h1, 1)
    far_mine, far_other, parts = forward(where, far, mine, other, False)
    r0, r1 = after((r0, r1), parts)
    sums_far = to_all_z(parts)
    b1, b2 = add_far(b1, b2, r0, r1)
    q1, q2 = from_z(b1, -1), from_z(b2, 1)
    near_got, far_got = from_core(near_other), from_core(far_other)
    trio_far = activate(sums_far)
    q1, q2 = after((q1, q2), trio_far)
    trio = activate(b0, q1, q2)
    t = trio.shape[1]
    up, down = from_z(trio, 1), from_z(trio, -1)
    trio_far, far0, far1 = backward(to_all_z(trio_far), mine, other, (2, 2))
    up, down = after((up, down), (far0, far1))
    far0, far1 = from_side(far0, -1), from_side(far1, 1)
    f0, f1 = from_z(down[:, : t // 2], -1), from_z(up[:, t // 2:], 1)
    trio_early, early = backward_early(trio, up, down, mine, other)
    f0, f1 = after((f0, f1), (far0, far1, early))
    trio_far_got, trio_early_got = (from_core(v) for v in after((trio_far, trio_early), f0))
    trio_late, line, ahead, behind = backward_late(where, f0, f1, early, far0, far1, mine, other, (4, 4, 4))
    trio_late_got = from_core(trio_late)

    ahead, behind = from_side(ahead, -1), from_side(behind, 1)

    rows = near_mine, far_mine, near_got, far_got
    trios = trio_early, trio_late, trio_far, trio_early_got, trio_late_got, trio_far_got
    gate_up = weights(rows, trios)
    ahead, behind = after((ahead, behind), gate_up)

    line = plus(line, ahead, behind)
    sent = [from_line(line[j].astype(BF), -OFFSETS[j]) for j in (3, 2, 1)]
    grad_w_down = down_weights(rows, trios)
    sent = after(sent, grad_w_down)
    sums = plus(line[0], *sent).astype(BF)
    got = from_core(sums[1])
    first = core == 0
    grad_tokens = jnp.concatenate([jnp.where(first, sums[0], got), jnp.where(first, got, sums[0])])
    return (grad_tokens, *gate_up, grad_w_down)


def solution(mesh):
    return jax.shard_map(
        local,
        mesh=mesh,
        in_specs=(P(XY, "inp"), P(XY, "inp"), P("inp", XY), P("inp", XY), P(XY, "inp")),
        out_specs=(P(XY, "inp"), P("inp", XY), P("inp", XY), P(XY, "inp")),
        check_vma=False,
    )
```
